128 devices in a mesh: tm: 8 (over x, z_hi), space: 16 (over y, z_lo, core).
Axes of the slice: x: 4, y: 4, z: 4 (z_hi: 2, z_lo: 2; z = z_hi * 2 + z_lo), core: 2. Of those that a mesh axis runs over, the one named last changes fastest.
Arguments:
- initial: float32 [4, 64, 16, 128], P(None, None, 'space'), may hold values from -6 to 6
- neighbours: int32 [6, 16, 128], P(None, 'space'), may hold values from 0 to 127, as said below
- step_counts: int32 [8], P('tm'), may hold values from 1 to 3
Outputs:
- node_states: float32 [8, 3, 4, 64, 16, 128], P('tm', None, None, None, 'space')
The draws below stay inside these ranges and needn't reach their ends.
Inputs may be any that keep to these rules, and one draw needn't show every extreme that they name: neighbours[f, i, e] is the element that shares face f (order -x, +x, -y, +y, -z, +z) with element e of layer i: an index in layer i-1 (f = 0) or i+1 (f = 1), periodic over 16 layers, or in layer i (f = 2..5). The elements of each layer form a periodic 8 x 16 grid, numbered in an order of that layer's own; the relation is symmetric and all elements keep the same orientation.
All inputs are finite; a program needn't handle non-finite values.
Results may differ from the reference program's by a relative error of at most 0.00014.
Values sent between devices are 32-bit elements; how exact they have to be, the bound alone decides.
No kernel may reach another device: no remote copies, remote signals or barrier semaphores. Data moves between devices by JAX's collectives and lax.ppermute only.
A program may use at most 64 MiB of HBM per device.

```python
import jax
import jax.numpy as jnp
import numpy as np
from jax import lax

FIELDS = 4
ORDER = 4
NODES = 64
ITERS = 2
EY = 8
EZ = 16
NEX = 16
SLICES = 8


def draw_neighbours(key, part):
    layer_keys = jax.random.split(key, NEX)

    def one_layer(layer_key):
        return jax.random.permutation(layer_key, EY * EZ).astype(jnp.int32)
    orders = jax.vmap(one_layer)(layer_keys)
    inverse = jnp.argsort(orders, axis=1).astype(jnp.int32)
    ycoord = orders // EZ
    zcoord = orders % EZ
    below_x = jnp.take_along_axis(jnp.roll(inverse, 1, axis=0), orders, axis=1)
    above_x = jnp.take_along_axis(jnp.roll(inverse, -1, axis=0), orders, axis=1)
    minus_y = jnp.take_along_axis(inverse, (ycoord + EY - 1) % EY * EZ + zcoord, axis=1)
    plus_y = jnp.take_along_axis(inverse, (ycoord + 1) % EY * EZ + zcoord, axis=1)
    minus_z = jnp.take_along_axis(inverse, ycoord * EZ + (zcoord + EZ - 1) % EZ, axis=1)
    plus_z = jnp.take_along_axis(inverse, ycoord * EZ + (zcoord + 1) % EZ, axis=1)
    return jnp.stack([below_x, above_x, minus_y, plus_y, minus_z, plus_z]).astype(jnp.int32)


def plant(drawn, stream_key, low, high):
    index_at = [jax.random.randint(jax.random.fold_in(stream_key, axis), (), 0, length) for axis, length in enumerate(drawn.shape)]
    main_axis = drawn.shape.index(max(drawn.shape))
    neighbour = index_at[:main_axis] + [(index_at[main_axis] + 1) % drawn.shape[main_axis]] + index_at[main_axis + 1:]
    return drawn.at[tuple(index_at)].set(low).at[tuple(neighbour)].set(high)


def block_scale(key, shape, cuts, low, top_value):
    def one(dim, blocks):
        draws = jax.random.uniform(jax.random.fold_in(jax.random.fold_in(key, 6), dim), (blocks,), jnp.float32, low / len(cuts), top_value / len(cuts))
        return jnp.repeat(jnp.exp(draws), shape[dim] // blocks).reshape((-1,) + (1,) * (len(shape) - dim - 1))

    factor_of = one(*cuts[0])
    for cut in cuts[1:]:
        factor_of = factor_of * one(*cut)
    return factor_of


def scatter_about(key, extent, width, bound, cuts=(), kind=jnp.bfloat16):
    values = width * jax.random.normal(key, extent, jnp.float32)
    if cuts:
        values = values * block_scale(key, extent, cuts, -0.22, 0.18)
    return jnp.clip(values, -bound, bound).astype(kind)


def setup_inputs(seed: int = 0) -> dict:
    arg_keys = jax.random.split(jax.random.key(seed), 4)
    initial = scatter_about(arg_keys[0], (FIELDS, NODES, NEX, EY * EZ), 1.0, 6.0, ((2, 16),), jnp.float32)
    neighbours = draw_neighbours(jax.random.fold_in(arg_keys[3], 71), 0)
    step_counts = plant(jax.random.randint(arg_keys[2], (SLICES,), 1, 4), jax.random.fold_in(arg_keys[2], 1), 1, 3).astype(jnp.int32)
    return dict(initial=initial, neighbours=neighbours, step_counts=step_counts)


LIFT_FACTOR = 6.0
BASE_STEP = 0.015

def derivative_table():
    points = np.array([-1.0, -1.0 / np.sqrt(5.0), 1.0 / np.sqrt(5.0), 1.0])
    node_count = points.shape[0]
    weights = np.zeros(node_count)
    for row_index in range(node_count):
        product = 1.0
        for col_index in range(node_count):
            if col_index != row_index:
                product = product * (points[row_index] - points[col_index])
        weights[row_index] = 1.0 / product
    table = np.zeros((node_count, node_count))
    for row_index in range(node_count):
        for col_index in range(node_count):
            if col_index != row_index:
                table[row_index, col_index] = weights[col_index] / weights[row_index] / (points[row_index] - points[col_index])
        table[row_index, row_index] = -np.sum(table[row_index])
    return table

def gather_faces(face, index):
    return jnp.take_along_axis(face, jnp.broadcast_to(index, face.shape), axis=-1)

def face_terms(inside, outside, sign, direction):
    jump_p = inside[:, 0] - outside[:, 0]
    jump_u = sign * (inside[:, direction] - outside[:, direction])
    return (0.5 * LIFT_FACTOR * (jump_u - jump_p), sign * 0.5 * LIFT_FACTOR * (jump_p - jump_u))

def apply_operator(field, low_outside, high_outside, neighbours, derivative):
    batch, fields, nodes, layers, cells = field.shape
    cube = field.reshape(batch, fields, ORDER, ORDER, ORDER, layers, cells)
    highest = lax.Precision.HIGHEST

    def along_x(value):
        return jnp.einsum('ia,kabcxe->kibcxe', derivative, value, precision=highest)

    def along_y(value):
        return jnp.einsum('ib,kabcxe->kaicxe', derivative, value, precision=highest)

    def along_z(value):
        return jnp.einsum('ic,kabcxe->kabixe', derivative, value, precision=highest)
    pressure = cube[:, 0]
    rate_p = -(along_x(cube[:, 1]) + along_y(cube[:, 2]) + along_z(cube[:, 3]))
    rate_x = -along_x(pressure)
    rate_y = -along_y(pressure)
    rate_z = -along_z(pressure)
    face_shape = (batch, fields, ORDER, ORDER, layers, cells)
    lower_out = gather_faces(low_outside.reshape(face_shape), neighbours[0])
    upper_out = gather_faces(high_outside.reshape(face_shape), neighbours[1])
    p_term, u_term = face_terms(cube[:, :, 0], lower_out, -1.0, 1)
    rate_p = rate_p.at[:, 0].add(p_term)
    rate_x = rate_x.at[:, 0].add(u_term)
    p_term, u_term = face_terms(cube[:, :, ORDER - 1], upper_out, 1.0, 1)
    rate_p = rate_p.at[:, ORDER - 1].add(p_term)
    rate_x = rate_x.at[:, ORDER - 1].add(u_term)
    p_term, u_term = face_terms(cube[:, :, :, 0], gather_faces(cube[:, :, :, ORDER - 1], neighbours[2]), -1.0, 2)
    rate_p = rate_p.at[:, :, 0].add(p_term)
    rate_y = rate_y.at[:, :, 0].add(u_term)
    p_term, u_term = face_terms(cube[:, :, :, ORDER - 1], gather_faces(cube[:, :, :, 0], neighbours[3]), 1.0, 2)
    rate_p = rate_p.at[:, :, ORDER - 1].add(p_term)
    rate_y = rate_y.at[:, :, ORDER - 1].add(u_term)
    p_term, u_term = face_terms(cube[:, :, :, :, 0], gather_faces(cube[:, :, :, :, ORDER - 1], neighbours[4]), -1.0, 3)
    rate_p = rate_p.at[:, :, :, 0].add(p_term)
    rate_z = rate_z.at[:, :, :, 0].add(u_term)
    p_term, u_term = face_terms(cube[:, :, :, :, ORDER - 1], gather_faces(cube[:, :, :, :, 0], neighbours[5]), 1.0, 3)
    rate_p = rate_p.at[:, :, :, ORDER - 1].add(p_term)
    rate_z = rate_z.at[:, :, :, ORDER - 1].add(u_term)
    rate = jnp.stack([rate_p, rate_x, rate_y, rate_z], axis=1)
    return rate.reshape(batch, fields, nodes, layers, cells)

def images(field, neighbours, derivative):
    quarter = NODES // ORDER
    low_outside = jnp.roll(field[:, :, NODES - quarter:], 1, axis=3)
    high_outside = jnp.roll(field[:, :, :quarter], -1, axis=3)
    return apply_operator(field, low_outside, high_outside, neighbours, derivative)

def reference(initial, neighbours, step_counts):
    derivative = jnp.asarray(derivative_table(), jnp.float32)
    slices = step_counts.shape[0]
    steps = step_counts.astype(jnp.float32) * BASE_STEP
    step_wide = steps[:, None, None, None, None]
    shape = initial.shape
    states = jnp.broadcast_to(initial[None, None], (slices, 3) + shape)
    for iteration in range(ITERS):
        old = images(states.reshape((slices * 3,) + shape), neighbours, derivative).reshape((slices, 3) + shape)
        start = states[:, 0]
        first = start + step_wide * (5.0 / 24.0 * old[:, 0] + 1.0 / 3.0 * old[:, 1] - 1.0 / 24.0 * old[:, 2])
        image_first = images(first, neighbours, derivative)
        second = first + step_wide * (image_first - old[:, 1]) + step_wide * (-1.0 / 24.0 * old[:, 0] + 1.0 / 3.0 * old[:, 1] + 5.0 / 24.0 * old[:, 2])
        image_second = images(second, neighbours, derivative)
        correction = step_wide * (2.0 / 3.0 * image_first - 1.0 / 3.0 * old[:, 0] - 1.0 / 3.0 * image_second)
        begin = initial
        begins = []
        finishes = []
        for position in range(slices):
            begin_image = images(begin[None], neighbours, derivative)[0]
            middle = begin + steps[position] * (begin_image - 0.5 * old[position, 0] + 0.5 * image_second[position]) + correction[position]
            middle_image = images(middle[None], neighbours, derivative)[0]
            finish = begin + 0.5 * steps[position] * (begin_image + middle_image) + correction[position]
            begins.append(begin)
            finishes.append(finish)
            begin = finish
        new_start = jnp.stack(begins)
        new_end = jnp.stack(finishes)
        middle_state = first + 0.5 * (new_start - start + (new_end - second))
        states = jnp.stack([new_start, middle_state, new_end], axis=1)
    return states
```

```python
import functools

import jax
import jax.numpy as jnp
import numpy as np
from jax import lax
from jax.experimental import pallas as pl
from jax.experimental.pallas import tpu as pltpu
from jax.sharding import PartitionSpec as P

ORDER = 4
NODES = 64
ITERS = 2
FIELDS = 4
SLICES = 8
LAYERS = 16
CELLS = 128
ROWS = FIELDS * NODES
PART = ROWS + 8
DEGREE = 22
BASE_STEP = 0.015

OFFSETS = (
    ((0, 1), ((2, 0), (2, 1))),
    ((1, 1), ((1, 0), (1, 1))),
    ((3, 1), ((3, 0), (3, 1))),
    ((1, 0), ((0, 0), (0, 0))),
    ((3, 0), ((0, 0), (0, 0))),
    ((2, 0), ((0, 0), (0, 0))),
    ((2, 1), ((0, 0), (0, 1))),
)


def modal_tables():
    points = np.array([-1.0, -1.0 / np.sqrt(5.0), 1.0 / np.sqrt(5.0), 1.0])
    to_nodes = np.polynomial.legendre.legvander(points, ORDER - 1)
    to_modes = np.linalg.inv(to_nodes)
    cube = lambda m: np.kron(np.kron(m, m), m).astype(np.float32)
    return cube(to_modes), cube(to_nodes)


def route(move):
    pairs = []
    for x in range(4):
        for high in range(2):
            for y in range(4):
                for low in range(2):
                    for core in range(2):
                        to_x, to_high, to_y, to_low, to_core = move(x, high, y, low, core)
                        source = (x * 2 + high) * 16 + y * 4 + low * 2 + core
                        target = (to_x % 4 * 2 + to_high % 2) * 16 + to_y % 4 * 4 + to_low % 2 * 2 + to_core % 2
                        pairs.append((source, target))
    return pairs


def prepare_kernel(step_ref, state_ref, near_ref, table_ref, out_ref):
    table = table_ref[...]
    for field in range(FIELDS):
        rows = pl.ds(field * NODES, NODES)
        out_ref[rows, :] = jnp.dot(
            table, state_ref[rows, :], precision=lax.Precision.HIGHEST, preferred_element_type=jnp.float32
        )
    near = near_ref[...].astype(jnp.float32)
    lane = lax.broadcasted_iota(jnp.int32, (2, CELLS), 1)
    count = jnp.where(lane == lax.axis_index("tm"), step_ref[0], 0).astype(jnp.float32)
    out_ref[pl.ds(ROWS, 8), :] = jnp.concatenate([near, count], axis=0)


def directional(p, u, fetch):
    o_u = u[1] + u[3]
    o_p = p[1] + p[3]
    m = (u[0] + u[2]) + o_p
    n = (p[0] + p[2]) + o_u
    x, y = m - n, m + n
    x_near, y_near = fetch(x, y)
    d_x = x_near - x
    d_y = y_near - y
    p_0 = 0.25 * (d_y - d_x)
    u_0 = 0.25 * (d_x + d_y)
    t = u_0 + o_p
    w = p_0 + o_u
    rate_p = [p_0, -3.0 * (t + u[2]), 5.0 * (p_0 + u[1]), -3.0 * t]
    rate_u = [u_0, -3.0 * (w + p[2]), 5.0 * (u_0 + p[1]), -3.0 * w]
    return rate_p, rate_u


def lanes(value, index):
    return jnp.take_along_axis(value, index, axis=1, mode="promise_in_bounds")


def row(field, a, b, c, v):
    return (field * NODES + a * 16 + b * 4 + c) * LAYERS + v * 8


def apply_operator(src, dst, index_ref):
    get = lambda r: src[pl.ds(r, 8), :]

    def put(r, value):
        dst[pl.ds(r, 8), :] = value

    index = lambda face, v: index_ref[pl.ds(face * LAYERS + v * 8, 8), :]
    four = range(ORDER)
    for b in four:
        for c in four:
            p = [[get(row(0, a, b, c, v)) for a in four] for v in range(2)]
            u = [[get(row(1, a, b, c, v)) for a in four] for v in range(2)]
            ends = []
            for v in range(2):
                o_u = u[v][1] + u[v][3]
                o_p = p[v][1] + p[v][3]
                m = (u[v][0] + u[v][2]) + o_p
                n = (p[v][0] + p[v][2]) + o_u
                ends.append((m - n, m + n))
            x_near = [lanes(ends[1][0], index(1, 0)), lanes(pltpu.roll(ends[0][0], 7, 0), index(1, 1))]
            y_near = [lanes(pltpu.roll(ends[1][1], 1, 0), index(0, 0)), lanes(ends[0][1], index(0, 1))]
            for v in range(2):
                rate_p, rate_u = directional(p[v], u[v], lambda x, y: (x_near[v], y_near[v]))
                for a in four:
                    put(row(0, a, b, c, v), rate_p[a])
                    put(row(1, a, b, c, v), rate_u[a])
    for v in range(2):
        for a in four:
            p = [[get(row(0, a, b, c, v)) for c in four] for b in four]
            rate = [[dst[pl.ds(row(0, a, b, c, v), 8), :] for c in four] for b in four]
            for c in four:
                u = [get(row(2, a, b, c, v)) for b in four]
                fetch = lambda x, y: (lanes(x, index(3, v)), lanes(y, index(2, v)))
                rate_p, rate_u = directional([p[b][c] for b in four], u, fetch)
                for b in four:
                    rate[b][c] = rate[b][c] + rate_p[b]
                    put(row(2, a, b, c, v), rate_u[b])
            for b in four:
                u = [get(row(3, a, b, c, v)) for c in four]
                fetch = lambda x, y: (lanes(x, index(5, v)), lanes(y, index(4, v)))
                rate_p, rate_u = directional(p[b], u, fetch)
                for c in four:
                    put(row(0, a, b, c, v), rate[b][c] + rate_p[c])
                    put(row(3, a, b, c, v), rate_u[c])


def coefficients(counts):
    rows = lax.broadcasted_iota(jnp.int32, (SLICES, CELLS), 0)
    lane = lax.broadcasted_iota(jnp.int32, (SLICES, CELLS), 1)
    wide = jnp.broadcast_to(counts, (SLICES, CELLS))
    h = jnp.sum(jnp.where(rows == lane, wide, 0.0), axis=1, keepdims=True) * BASE_STEP
    h = jnp.broadcast_to(h, (SLICES, CELLS))
    image = lambda value: pltpu.roll(value, 1, 1)
    initial = jnp.where(lane == 0, 1.0, 0.0)
    spread = lambda value, n: jnp.broadcast_to(value[n : n + 1], (SLICES, CELLS))
    u_0 = u_1 = u_2 = initial
    for _ in range(ITERS):
        old_0, old_1, old_2 = image(u_0), image(u_1), image(u_2)
        first = u_0 + h * (5.0 / 24.0 * old_0 + 1.0 / 3.0 * old_1 - 1.0 / 24.0 * old_2)
        image_first = image(first)
        second = (
            first
            + h * (image_first - old_1)
            + h * (-1.0 / 24.0 * old_0 + 1.0 / 3.0 * old_1 + 5.0 / 24.0 * old_2)
        )
        image_second = image(second)
        correction = h * (2.0 / 3.0 * image_first - 1.0 / 3.0 * old_0 - 1.0 / 3.0 * image_second)
        carried = h * (0.5 * image_second - 0.5 * old_0) + correction
        begin = initial
        begins = initial
        finishes = initial
        for n in range(SLICES):
            h_n = spread(h, n)
            begin_image = image(begin)
            middle_image = image(begin + h_n * begin_image + spread(carried, n))
            finish = begin + 0.5 * h_n * (begin_image + middle_image) + spread(correction, n)
            begins = jnp.where(rows == n, begin, begins)
            finishes = jnp.where(rows == n, finish, finishes)
            begin = finish
        u_1 = first + 0.5 * ((begins - u_0) + (finishes - second))
        u_0, u_2 = begins, finishes
    return u_0, u_1, u_2


def advance_kernel(*refs):
    parts = refs[:LAYERS]
    table_ref, out_ref, one, two, index_ref, saved, coef_ref, spread_ref, sum_ref = refs[LAYERS:]
    space = lax.axis_index("space")
    core = space % 2
    chip = space // 2
    low = chip % 2
    high = chip // 2
    place = lambda layer: (layer % 2) * 8 + layer // 2
    counts = jnp.zeros((1, CELLS), jnp.float32)
    for k, part in enumerate(parts):
        offset = ((0, 0),) + tuple(o for o, _ in OFFSETS)
        step_y, step_z = offset[k % 8]
        from_y = (high + 4 - step_y) % 4
        from_z = (low + step_z) % 2
        layer = from_y * 4 + from_z * 2 + (core if k < 8 else 1 - core)
        base = place(layer)
        for m in range(ROWS // 8):
            one[pl.ds(m * 8 * LAYERS + base, 8, stride=LAYERS), :] = part[pl.ds(m * 8, 8), :]
        tail = part[pl.ds(ROWS, 8), :]
        for face in range(6):
            index_ref[pl.ds(face * LAYERS + base, 1), :] = tail[face : face + 1].astype(jnp.int32)
        counts = jnp.maximum(counts, tail[6:7])

    polynomials = coefficients(counts)
    for m in range(3):
        coef_ref[pl.ds(m * 8, 8), :] = polynomials[m]
    own_slice = lax.axis_index("tm")
    for m in range(3):
        mine = jnp.broadcast_to(coef_ref[pl.ds(m * 8 + own_slice, 1), :], (8, CELLS))
        for k in range(DEGREE + 1):
            spread_ref[pl.ds((k * 3 + m) * 8, 8), :] = jnp.broadcast_to(mine[:, k : k + 1], (8, CELLS))

    own = place(space)

    def keep(source, k):
        for m in range(ROWS // 8):
            saved[pl.ds(k * ROWS + m * 8, 8), :] = source[pl.ds(m * 8 * LAYERS + own, 8, stride=LAYERS), :]

    keep(one, 0)

    def advance(turn, carry):
        apply_operator(one, two, index_ref)
        keep(two, 2 * turn + 1)
        apply_operator(two, one, index_ref)
        keep(one, 2 * turn + 2)
        return carry

    lax.fori_loop(0, DEGREE // 2, advance, 0)

    group = 16

    def combine(g, carry):
        total = [[None] * group for _ in range(3)]
        for k in range(DEGREE + 1):
            value = [saved[pl.ds(k * ROWS + (g * group + i) * 8, 8), :] for i in range(group)]
            for m in range(3):
                factor = spread_ref[pl.ds((k * 3 + m) * 8, 8), :]
                for i in range(group):
                    term = factor * value[i]
                    total[m][i] = term if total[m][i] is None else total[m][i] + term
        for m in range(3):
            for i in range(group):
                sum_ref[pl.ds(m * ROWS + (g * group + i) * 8, 8), :] = total[m][i]
        return carry

    lax.fori_loop(0, ROWS // 8 // group, combine, 0)
    table = table_ref[...]
    for m in range(3 * FIELDS):
        rows = pl.ds(m * NODES, NODES)
        out_ref[rows, :] = jnp.dot(
            table, sum_ref[rows, :], precision=lax.Precision.HIGHEST, preferred_element_type=jnp.float32
        )


def shards(initial, neighbours, step_counts):
    to_modes, to_nodes = modal_tables()
    state = initial.reshape(ROWS, CELLS)
    near = neighbours.reshape(6, CELLS)
    whole = lambda: pl.BlockSpec(memory_space=pltpu.VMEM)
    part = pl.pallas_call(
        prepare_kernel,
        out_shape=jax.ShapeDtypeStruct((PART, CELLS), jnp.float32),
        in_specs=[pl.BlockSpec(memory_space=pltpu.SMEM), whole(), whole(), whole()],
        out_specs=whole(),
    )(step_counts, state, near, jnp.asarray(to_modes))

    axes = ("tm", "space")
    parts = [part]
    for (step_y, step_z), skew in OFFSETS:

        def move(x, high, y, low, core):
            return (x + skew[core][0], high + skew[core][1], y + step_y, low + step_z, core)

        parts.append(lax.ppermute(part, axes, route(move)))
    swap = route(lambda x, high, y, low, core: (x, high, y, low, core + 1))
    parts += [lax.ppermute(value, axes, swap) for value in parts]

    result = pl.pallas_call(
        advance_kernel,
        out_shape=jax.ShapeDtypeStruct((3 * ROWS, CELLS), jnp.float32),
        in_specs=[whole() for _ in range(LAYERS + 1)],
        out_specs=whole(),
        scratch_shapes=[
            pltpu.VMEM((ROWS * LAYERS, CELLS), jnp.float32),
            pltpu.VMEM((ROWS * LAYERS, CELLS), jnp.float32),
            pltpu.VMEM((6 * LAYERS, CELLS), jnp.int32),
            pltpu.VMEM(((DEGREE + 1) * ROWS, CELLS), jnp.float32),
            pltpu.VMEM((24, CELLS), jnp.float32),
            pltpu.VMEM(((DEGREE + 1) * 3 * 8, CELLS), jnp.float32),
            pltpu.VMEM((3 * ROWS, CELLS), jnp.float32),
        ],
        compiler_params=pltpu.CompilerParams(vmem_limit_bytes=32 * 1024 * 1024),
    )(*parts, jnp.asarray(to_nodes))
    return result.reshape(1, 3, FIELDS, NODES, 1, CELLS)


def solution(mesh):
    placed = (P(None, None, "space", None), P(None, "space", None), P("tm"))
    return jax.shard_map(
        shards,
        mesh=mesh,
        in_specs=placed,
        out_specs=P("tm", None, None, None, "space", None),
        check_vma=False,
    )
```

```python
import jax
import jax.numpy as jnp
import numpy as np
from jax import lax
from jax.experimental import pallas as pl
from jax.experimental.pallas import tpu as pltpu
from jax.sharding import PartitionSpec as P

ORDER = 4
NODES = 64
ITERS = 2
FIELDS = 4
SLICES = 8
LAYERS = 16
CELLS = 128
ROWS = FIELDS * NODES
PART = ROWS + 8
PAIR = 2 * PART + 8
DEGREE = 22
BASE_STEP = 0.015

OFFSETS = (
    (((2, 1), (0, 0)), ((2, 0), (0, 0))),
    (((1, 0), (0, 0)), ((3, 0), (0, 0))),
    (((1, 1), (1, 1)), ((3, 1), (1, 0))),
    (((0, 1), (0, 1)), None),
)
EARLY = 2


def modal_tables():
    points = np.array([-1.0, -1.0 / np.sqrt(5.0), 1.0 / np.sqrt(5.0), 1.0])
    to_nodes = np.polynomial.legendre.legvander(points, ORDER - 1)
    to_modes = np.linalg.inv(to_nodes)
    cube = lambda m: np.kron(np.kron(m, m), m).astype(np.float32)
    return cube(to_modes), cube(to_nodes)


def route(move):
    pairs = []
    for x in range(4):
        for high in range(2):
            for y in range(4):
                for low in range(2):
                    for core in range(2):
                        target = move(x, high, y, low, core)
                        if target is None:
                            continue
                        to_x, to_high, to_y, to_low, to_core = target
                        source = (x * 2 + high) * 16 + y * 4 + low * 2 + core
                        place = (to_x % 4 * 2 + to_high % 2) * 16 + to_y % 4 * 4 + to_low % 2 * 2 + to_core % 2
                        pairs.append((source, place))
    return pairs


def prepare_kernel(step_ref, state_ref, other_ref, near_ref, near_other_ref, table_ref, out_ref, copy_ref):
    table = table_ref[...]
    core = lax.axis_index("space") % 2
    for k, (state, near) in enumerate(((state_ref, near_ref), (other_ref, near_other_ref))):
        base = pl.multiple_of((core if k == 0 else 1 - core) * PART, 8)
        for field in range(FIELDS):
            value = jnp.dot(
                table,
                state[pl.ds(field * NODES, NODES), :],
                precision=lax.Precision.HIGHEST,
                preferred_element_type=jnp.float32,
            )
            rows = pl.ds(base + field * NODES, NODES)
            out_ref[rows, :] = value
            copy_ref[rows, :] = value
        tail = jnp.concatenate([near[f].astype(jnp.float32) for f in (0, 1, 2, 3, 4, 5, 5, 5)], axis=0)
        rows = pl.ds(base + ROWS, 8)
        out_ref[rows, :] = tail
        copy_ref[rows, :] = tail
    lane = lax.broadcasted_iota(jnp.int32, (8, CELLS), 1)
    count = jnp.where(lane == lax.axis_index("tm"), step_ref[0], 0).astype(jnp.float32)
    out_ref[pl.ds(2 * PART, 8), :] = count
    copy_ref[pl.ds(2 * PART, 8), :] = count


def count_kernel(step_ref, far_ref, pair_any, out_any, counts, sem):
    lane = lax.broadcasted_iota(jnp.int32, (8, CELLS), 1)
    own = lax.axis_index("tm")
    far = (own // 2 + 2) % 4 * 2 + own % 2
    count = jnp.where(lane == own, step_ref[0], jnp.where(lane == far, far_ref[0], 0))
    counts[...] = count.astype(jnp.float32)
    copy = pltpu.make_async_copy(counts, out_any.at[pl.ds(2 * PART, 8), :], sem)
    copy.start()
    copy.wait()


def ends(p, u):
    m = (u[0] + u[2]) + (p[1] + p[3])
    n = (p[0] + p[2]) + (u[1] + u[3])
    return m - n, m + n


def rates(p, u, d_x, d_y):
    o_u = u[1] + u[3]
    o_p = p[1] + p[3]
    p_0 = 0.25 * (d_y - d_x)
    u_0 = 0.25 * (d_x + d_y)
    t = u_0 + o_p
    w = p_0 + o_u
    rate_p = [p_0, -3.0 * (t + u[2]), 5.0 * (p_0 + u[1]), -3.0 * t]
    rate_u = [u_0, -3.0 * (w + p[2]), 5.0 * (u_0 + p[1]), -3.0 * w]
    return rate_p, rate_u


def lanes(value, index):
    return jnp.take_along_axis(value, index, axis=1, mode="promise_in_bounds")


def row(field, a, b, c, v):
    return (field * NODES + a * 16 + b * 4 + c) * LAYERS + v * 8


def apply_operator(src, dst, index_ref):
    get = lambda r: src[pl.ds(r, 8), :]

    def put(r, value):
        dst[pl.ds(r, 8), :] = value

    index = lambda face, v: index_ref[pl.ds(face * LAYERS + v * 8, 8), :]
    four = range(ORDER)
    for b in four:
        low = [[ends([get(row(0, a, b, c, v)) for a in four], [get(row(1, a, b, c, v)) for a in four]) for c in four] for v in range(2)]
        near_x = [
            [lanes(low[1][c][0], index(1, 0)) for c in four],
            [lanes(pltpu.roll(low[0][c][0], 7, 0), index(1, 1)) for c in four],
        ]
        near_y = [
            [lanes(pltpu.roll(low[1][c][1], 1, 0), index(0, 0)) for c in four],
            [lanes(low[0][c][1], index(0, 1)) for c in four],
        ]
        for v in range(2):
            for c in four:
                p = [get(row(0, a, b, c, v)) for a in four]
                u = [get(row(1, a, b, c, v)) for a in four]
                rate_p, rate_u = rates(p, u, near_x[v][c] - low[v][c][0], near_y[v][c] - low[v][c][1])
                for a in four:
                    put(row(0, a, b, c, v), rate_p[a])
                    put(row(1, a, b, c, v), rate_u[a])
    for v in range(2):
        for a in four:
            rate = [[None] * ORDER for _ in four]
            column = lambda c: ([get(row(0, a, b, c, v)) for b in four], [get(row(2, a, b, c, v)) for b in four])
            line = lambda b: ([get(row(0, a, b, c, v)) for c in four], [get(row(3, a, b, c, v)) for c in four])
            low_y = [ends(*column(c)) for c in four]
            low_z = [ends(*line(b)) for b in four]
            x_y = [lanes(low_y[c][0], index(3, v)) - low_y[c][0] for c in four]
            y_y = [lanes(low_y[c][1], index(2, v)) - low_y[c][1] for c in four]
            x_z = [lanes(low_z[b][0], index(5, v)) - low_z[b][0] for b in four]
            y_z = [lanes(low_z[b][1], index(4, v)) - low_z[b][1] for b in four]
            for c in four:
                rate_p, rate_u = rates(*column(c), x_y[c], y_y[c])
                for b in four:
                    rate[b][c] = rate_p[b]
                    put(row(2, a, b, c, v), rate_u[b])
            for b in four:
                rate_p, rate_u = rates(*line(b), x_z[b], y_z[b])
                for c in four:
                    r = row(0, a, b, c, v)
                    put(r, dst[pl.ds(r, 8), :] + (rate[b][c] + rate_p[c]))
                    put(row(3, a, b, c, v), rate_u[c])


def coefficients(counts):
    lane = lax.broadcasted_iota(jnp.int32, (8, CELLS), 1)
    wide = jnp.broadcast_to(counts, (8, CELLS))
    steps = [jnp.broadcast_to(wide[:, n : n + 1], (8, CELLS)) * BASE_STEP for n in range(SLICES)]
    image = lambda value: pltpu.roll(value, 1, 1)
    twice = lambda value: pltpu.roll(value, 2, 1)
    initial = jnp.where(lane == 0, 1.0, 0.0)
    states = [(initial, initial, initial)] * SLICES
    for _ in range(ITERS):
        begin = initial
        fresh = []
        for n in range(SLICES):
            h = steps[n]
            u_0, u_1, u_2 = states[n]
            old_0, old_1, old_2 = image(u_0), image(u_1), image(u_2)
            first = u_0 + h * (5.0 / 24.0 * old_0 + 1.0 / 3.0 * old_1 - 1.0 / 24.0 * old_2)
            image_first = image(first)
            second = (
                first
                + h * (image_first - old_1)
                + h * (-1.0 / 24.0 * old_0 + 1.0 / 3.0 * old_1 + 5.0 / 24.0 * old_2)
            )
            image_second = image(second)
            correction = h * (2.0 / 3.0 * image_first - 1.0 / 3.0 * old_0 - 1.0 / 3.0 * image_second)
            carried = h * (0.5 * image_second - 0.5 * old_0) + correction
            offset = 0.5 * h * image(carried) + correction
            finish = begin + h * image(begin) + 0.5 * h * h * twice(begin) + offset
            fresh.append((begin, first + 0.5 * ((begin - u_0) + (finish - second)), finish))
            begin = finish
        states = fresh
    return states


def advance_kernel(*refs):
    pairs = refs[:9]
    table_ref, out_ref, one, two, index_ref, saved, coef_ref, spread_ref, sum_ref = refs[9:]
    space = lax.axis_index("space")
    core = space % 2
    chip = space // 2
    low = chip % 2
    high = chip // 2
    counts = jnp.zeros((1, CELLS), jnp.float32)

    def take(pair, step_y, step_z):
        place = (high + 4 - step_y) % 4 * 2 + (low + step_z) % 2
        for half in range(2):
            base = place + 8 * half
            for m in range(ROWS // 8):
                one[pl.ds(m * 8 * LAYERS + base, 8, stride=LAYERS), :] = pair[pl.ds(half * PART + m * 8, 8), :]
            tail = pair[pl.ds(half * PART + ROWS, 8), :]
            for face in range(6):
                index_ref[pl.ds(face * LAYERS + base, 1), :] = tail[face : face + 1].astype(jnp.int32)

    take(pairs[0], 0, 0)
    for k, (zero, first) in enumerate(OFFSETS):
        if first is None:

            @pl.when(core == 0)
            def _():
                take(pairs[1 + k], *zero[0])

            @pl.when(core == 1)
            def _():
                take(pairs[5 + k], *zero[0])
        else:
            for swapped in range(2):
                on_zero = core == swapped
                step_y = jnp.where(on_zero, zero[0][0], first[0][0])
                step_z = jnp.where(on_zero, zero[0][1], first[0][1])
                take(pairs[1 + 4 * swapped + k], step_y, step_z)
    for pair in pairs:
        counts = jnp.maximum(counts, pair[pl.ds(2 * PART, 1), :])

    polynomials = coefficients(counts)
    for n in range(SLICES):
        for m in range(3):
            coef_ref[pl.ds((n * 3 + m) * 8, 8), :] = polynomials[n][m]
    own_slice = lax.axis_index("tm")
    for m in range(3):
        mine = coef_ref[pl.ds(pl.multiple_of((own_slice * 3 + m) * 8, 8), 8), :]
        for k in range(DEGREE + 1):
            spread_ref[pl.ds((k * 3 + m) * 8, 8), :] = jnp.broadcast_to(mine[:, k : k + 1], (8, CELLS))

    own = core * 8 + chip

    def keep(source, k):
        for m in range(ROWS // 8):
            saved[pl.ds(k * ROWS + m * 8, 8), :] = source[pl.ds(m * 8 * LAYERS + own, 8, stride=LAYERS), :]

    keep(one, 0)

    def advance(turn, carry):
        apply_operator(one, two, index_ref)
        keep(two, 2 * turn + 1)
        apply_operator(two, one, index_ref)
        keep(one, 2 * turn + 2)
        return carry

    lax.fori_loop(0, DEGREE // 2, advance, 0)

    group = 16

    def combine(g, carry):
        total = [[None] * group for _ in range(3)]
        for k in range(DEGREE + 1):
            value = [saved[pl.ds(k * ROWS + (g * group + i) * 8, 8), :] for i in range(group)]
            for m in range(3):
                factor = spread_ref[pl.ds((k * 3 + m) * 8, 8), :]
                for i in range(group):
                    term = factor * value[i]
                    total[m][i] = term if total[m][i] is None else total[m][i] + term
        for m in range(3):
            for i in range(group):
                sum_ref[pl.ds(m * ROWS + (g * group + i) * 8, 8), :] = total[m][i]
        return carry

    lax.fori_loop(0, ROWS // 8 // group, combine, 0)
    table = table_ref[...]
    for m in range(3 * FIELDS):
        rows = pl.ds(m * NODES, NODES)
        out_ref[rows, :] = jnp.dot(
            table, sum_ref[rows, :], precision=lax.Precision.HIGHEST, preferred_element_type=jnp.float32
        )


def shards(initial, neighbours, step_counts):
    to_modes, to_nodes = modal_tables()
    axes = ("tm", "space")
    swap = route(lambda x, high, y, low, core: (x, high, y, low, core + 1))
    one_way = route(lambda x, high, y, low, core: (x, high, y, low, 1) if core == 0 else None)
    far = lax.ppermute(step_counts, axes, route(lambda x, high, y, low, core: (x + 2, high, y, low, core)))
    state = initial.reshape(ROWS, CELLS)
    other = lax.ppermute(state, axes, swap)
    near_other = lax.ppermute(neighbours, axes, swap)
    whole = lambda: pl.BlockSpec(memory_space=pltpu.VMEM)
    anywhere = lambda: pl.BlockSpec(memory_space=pl.ANY)
    scalar = lambda: pl.BlockSpec(memory_space=pltpu.SMEM)
    pair, late = pl.pallas_call(
        prepare_kernel,
        out_shape=[jax.ShapeDtypeStruct((PAIR, CELLS), jnp.float32)] * 2,
        in_specs=[scalar()] + [whole() for _ in range(5)],
        out_specs=[whole(), whole()],
    )(step_counts, state, other, neighbours, near_other, jnp.asarray(to_modes))
    late = pl.pallas_call(
        count_kernel,
        out_shape=jax.ShapeDtypeStruct((PAIR, CELLS), jnp.float32),
        in_specs=[scalar(), scalar(), anywhere()],
        out_specs=anywhere(),
        scratch_shapes=[pltpu.VMEM((8, CELLS), jnp.float32), pltpu.SemaphoreType.DMA],
        input_output_aliases={2: 0},
    )(step_counts, far, late)

    direct = []
    for k, entry in enumerate(OFFSETS):

        def move(x, high, y, low, core):
            if entry[core] is None:
                return None
            (step_y, step_z), (skew_x, skew_z) = entry[core]
            return (x + skew_x, high + skew_z, y + step_y, low + step_z, core)

        direct.append(lax.ppermute(pair if k < EARLY else late, axes, route(move)))
    own = lax.ppermute(late, axes, swap)
    swapped = [
        lax.ppermute(value, axes, one_way if entry[1] is None else swap) for value, entry in zip(direct, OFFSETS)
    ]
    pairs = [own] + direct + swapped

    result = pl.pallas_call(
        advance_kernel,
        out_shape=jax.ShapeDtypeStruct((3 * ROWS, CELLS), jnp.float32),
        in_specs=[whole() for _ in range(10)],
        out_specs=whole(),
        scratch_shapes=[
            pltpu.VMEM((ROWS * LAYERS, CELLS), jnp.float32),
            pltpu.VMEM((ROWS * LAYERS, CELLS), jnp.float32),
            pltpu.VMEM((6 * LAYERS, CELLS), jnp.int32),
            pltpu.VMEM(((DEGREE + 1) * ROWS, CELLS), jnp.float32),
            pltpu.VMEM((SLICES * 3 * 8, CELLS), jnp.float32),
            pltpu.VMEM(((DEGREE + 1) * 3 * 8, CELLS), jnp.float32),
            pltpu.VMEM((3 * ROWS, CELLS), jnp.float32),
        ],
        compiler_params=pltpu.CompilerParams(vmem_limit_bytes=32 * 1024 * 1024),
    )(*pairs, jnp.asarray(to_nodes))
    return result.reshape(1, 3, FIELDS, NODES, 1, CELLS)


def solution(mesh):
    placed = (P(None, None, "space", None), P(None, "space", None), P("tm"))
    return jax.shard_map(
        shards,
        mesh=mesh,
        in_specs=placed,
        out_specs=P("tm", None, None, None, "space", None),
        check_vma=False,
    )
```

```python
import functools

import jax
import jax.numpy as jnp
import numpy as np
from jax import lax
from jax.experimental import pallas as pl
from jax.experimental.pallas import tpu as pltpu
from jax.sharding import PartitionSpec as P

ORDER = 4
NODES = 64
ITERS = 2
FIELDS = 4
SLICES = 8
LAYERS = 16
CELLS = 128
ROWS = FIELDS * NODES
PART = ROWS + 8
PAIR = 2 * PART + 8
DEGREE = 22
BASE_STEP = 0.015

OFFSETS = (
    (((2, 1), (0, 0)), ((2, 0), (0, 0))),
    (((1, 0), (0, 0)), ((3, 0), (0, 0))),
    (((1, 1), (1, 1)), ((3, 1), (1, 0))),
    (((0, 1), (0, 1)), None),
)
EARLY = 2


def modal_tables():
    points = np.array([-1.0, -1.0 / np.sqrt(5.0), 1.0 / np.sqrt(5.0), 1.0])
    to_nodes = np.polynomial.legendre.legvander(points, ORDER - 1)
    to_modes = np.linalg.inv(to_nodes)
    cube = lambda m: np.kron(np.kron(m, m), m).astype(np.float32)
    return cube(to_modes), cube(to_nodes)


def route(move):
    pairs = []
    for x in range(4):
        for high in range(2):
            for y in range(4):
                for low in range(2):
                    for core in range(2):
                        target = move(x, high, y, low, core)
                        if target is None:
                            continue
                        to_x, to_high, to_y, to_low, to_core = target
                        source = (x * 2 + high) * 16 + y * 4 + low * 2 + core
                        place = (to_x % 4 * 2 + to_high % 2) * 16 + to_y % 4 * 4 + to_low % 2 * 2 + to_core % 2
                        pairs.append((source, place))
    return pairs


def prepare_kernel(step_ref, state_ref, other_ref, near_ref, near_other_ref, table_ref, out_ref, copy_ref):
    table = table_ref[...]
    core = lax.axis_index("space") % 2
    for k, (state, near) in enumerate(((state_ref, near_ref), (other_ref, near_other_ref))):
        base = pl.multiple_of((core if k == 0 else 1 - core) * PART, 8)
        for field in range(FIELDS):
            value = jnp.dot(
                table,
                state[pl.ds(field * NODES, NODES), :],
                precision=lax.Precision.HIGHEST,
                preferred_element_type=jnp.float32,
            )
            rows = pl.ds(base + field * NODES, NODES)
            out_ref[rows, :] = value
            copy_ref[rows, :] = value
        tail = jnp.concatenate([near[f].astype(jnp.float32) for f in (0, 1, 2, 3, 4, 5, 5, 5)], axis=0)
        rows = pl.ds(base + ROWS, 8)
        out_ref[rows, :] = tail
        copy_ref[rows, :] = tail
    lane = lax.broadcasted_iota(jnp.int32, (8, CELLS), 1)
    count = jnp.where(lane == lax.axis_index("tm"), step_ref[0], 0).astype(jnp.float32)
    out_ref[pl.ds(2 * PART, 8), :] = count
    copy_ref[pl.ds(2 * PART, 8), :] = count


def count_kernel(step_ref, far_ref, pair_any, out_any, counts, sem):
    lane = lax.broadcasted_iota(jnp.int32, (8, CELLS), 1)
    own = lax.axis_index("tm")
    far = (own // 2 + 2) % 4 * 2 + own % 2
    count = jnp.where(lane == own, step_ref[0], jnp.where(lane == far, far_ref[0], 0))
    counts[...] = count.astype(jnp.float32)
    copy = pltpu.make_async_copy(counts, out_any.at[pl.ds(2 * PART, 8), :], sem)
    copy.start()
    copy.wait()


def ends(p, u):
    o_p, o_u = p[1] + p[3], u[1] + u[3]
    m = (u[0] + u[2]) + o_p
    n = (p[0] + p[2]) + o_u
    return m - n, m + n, o_p, o_u


def rates(p, u, near_x, near_y, end):
    x, y, o_p, o_u = end
    d_x = near_x - x
    d_y = near_y - y
    p_0 = 0.25 * (d_y - d_x)
    u_0 = 0.25 * (d_x + d_y)
    t = u_0 + o_p
    w = p_0 + o_u
    rate_p = [p_0, -3.0 * (t + u[1]), 5.0 * (p_0 + u[0]), -3.0 * t]
    rate_u = [u_0, -3.0 * (w + p[1]), 5.0 * (u_0 + p[0]), -3.0 * w]
    return rate_p, rate_u


def lanes(value, index):
    return jnp.take_along_axis(value, index, axis=1, mode="promise_in_bounds")


def row(field, a, b, c, v):
    return (field * NODES + a * 16 + b * 4 + c) * LAYERS + v * 8


def apply_operator(src, dst, index_ref):
    get = lambda r: src[pl.ds(r, 8), :]

    def put(r, value):
        dst[pl.ds(r, 8), :] = value

    index = lambda face, v: index_ref[pl.ds(face * LAYERS + v * 8, 8), :]
    four = range(ORDER)
    middle = (1, 2)
    for b in four:
        end = [
            [ends([get(row(0, a, b, c, v)) for a in four], [get(row(1, a, b, c, v)) for a in four]) for c in four]
            for v in range(2)
        ]
        near_x = [
            [lanes(end[1][c][0], index(1, 0)) for c in four],
            [lanes(pltpu.roll(end[0][c][0], 7, 0), index(1, 1)) for c in four],
        ]
        near_y = [
            [lanes(pltpu.roll(end[1][c][1], 1, 0), index(0, 0)) for c in four],
            [lanes(end[0][c][1], index(0, 1)) for c in four],
        ]
        for v in range(2):
            for c in four:
                p = [get(row(0, a, b, c, v)) for a in middle]
                u = [get(row(1, a, b, c, v)) for a in middle]
                rate_p, rate_u = rates(p, u, near_x[v][c], near_y[v][c], end[v][c])
                for a in four:
                    put(row(0, a, b, c, v), rate_p[a])
                    put(row(1, a, b, c, v), rate_u[a])
    for v in range(2):
        for a in four:
            p = [[get(row(0, a, b, c, v)) for c in four] for b in four]
            rate = [[None] * ORDER for _ in four]
            end = [ends([p[b][c] for b in four], [get(row(2, a, b, c, v)) for b in four]) for c in four]
            near_x = [lanes(end[c][0], index(3, v)) for c in four]
            near_y = [lanes(end[c][1], index(2, v)) for c in four]
            for c in four:
                u = [get(row(2, a, b, c, v)) for b in middle]
                rate_p, rate_u = rates([p[b][c] for b in middle], u, near_x[c], near_y[c], end[c])
                for b in four:
                    rate[b][c] = rate_p[b]
                    put(row(2, a, b, c, v), rate_u[b])
            end = [ends(p[b], [get(row(3, a, b, c, v)) for c in four]) for b in four]
            near_x = [lanes(end[b][0], index(5, v)) for b in four]
            near_y = [lanes(end[b][1], index(4, v)) for b in four]
            for b in four:
                u = [get(row(3, a, b, c, v)) for c in middle]
                rate_p, rate_u = rates([p[b][c] for c in middle], u, near_x[b], near_y[b], end[b])
                for c in four:
                    r = row(0, a, b, c, v)
                    put(r, dst[pl.ds(r, 8), :] + (rate[b][c] + rate_p[c]))
                    put(row(3, a, b, c, v), rate_u[c])


def coefficients(counts):
    lane = lax.broadcasted_iota(jnp.int32, (8, CELLS), 1)
    wide = jnp.broadcast_to(counts, (8, CELLS))
    steps = [jnp.broadcast_to(wide[:, n : n + 1], (8, CELLS)) * BASE_STEP for n in range(SLICES)]
    image = lambda value: pltpu.roll(value, 1, 1)
    twice = lambda value: pltpu.roll(value, 2, 1)
    initial = jnp.where(lane == 0, 1.0, 0.0)
    states = [(initial, initial, initial)] * SLICES
    for _ in range(ITERS):
        begin = initial
        fresh = []
        for n in range(SLICES):
            h = steps[n]
            u_0, u_1, u_2 = states[n]
            old_0, old_1, old_2 = image(u_0), image(u_1), image(u_2)
            first = u_0 + h * (5.0 / 24.0 * old_0 + 1.0 / 3.0 * old_1 - 1.0 / 24.0 * old_2)
            image_first = image(first)
            second = (
                first
                + h * (image_first - old_1)
                + h * (-1.0 / 24.0 * old_0 + 1.0 / 3.0 * old_1 + 5.0 / 24.0 * old_2)
            )
            image_second = image(second)
            correction = h * (2.0 / 3.0 * image_first - 1.0 / 3.0 * old_0 - 1.0 / 3.0 * image_second)
            carried = h * (0.5 * image_second - 0.5 * old_0) + correction
            offset = 0.5 * h * image(carried) + correction
            finish = begin + h * image(begin) + 0.5 * h * h * twice(begin) + offset
            fresh.append((begin, first + 0.5 * ((begin - u_0) + (finish - second)), finish))
            begin = finish
        states = fresh
    return states


def advance_kernel(*refs):
    pairs = refs[:9]
    table_ref, out_ref, one, two, index_ref, saved, coef_ref, spread_ref, sum_ref = refs[9:]
    space = lax.axis_index("space")
    core = space % 2
    chip = space // 2
    low = chip % 2
    high = chip // 2
    counts = jnp.zeros((1, CELLS), jnp.float32)

    def take(read, step_y, step_z):
        place = (high + 4 - step_y) % 4 * 2 + (low + step_z) % 2
        for half in range(2):
            base = place + 8 * half
            for m in range(ROWS // 8):
                one[pl.ds(m * 8 * LAYERS + base, 8, stride=LAYERS), :] = read(half * PART + m * 8)
            tail = read(half * PART + ROWS)
            for face in range(6):
                index_ref[pl.ds(face * LAYERS + base, 1), :] = tail[face : face + 1].astype(jnp.int32)

    def reader(*sources):
        return lambda r: functools.reduce(jnp.add, [source[pl.ds(r, 8), :] for source in sources])

    take(reader(pairs[0]), 0, 0)
    for k, (zero, first) in enumerate(OFFSETS):
        if first is None:
            take(reader(pairs[1 + k], pairs[5 + k]), *zero[0])
        else:
            for swapped in range(2):
                on_zero = core == swapped
                step_y = jnp.where(on_zero, zero[0][0], first[0][0])
                step_z = jnp.where(on_zero, zero[0][1], first[0][1])
                take(reader(pairs[1 + 4 * swapped + k]), step_y, step_z)
    for pair in pairs:
        counts = jnp.maximum(counts, pair[pl.ds(2 * PART, 1), :])

    polynomials = coefficients(counts)
    for n in range(SLICES):
        for m in range(3):
            coef_ref[pl.ds((n * 3 + m) * 8, 8), :] = polynomials[n][m]
    own_slice = lax.axis_index("tm")
    for m in range(3):
        mine = coef_ref[pl.ds(pl.multiple_of((own_slice * 3 + m) * 8, 8), 8), :]
        for k in range(DEGREE + 1):
            spread_ref[pl.ds((k * 3 + m) * 8, 8), :] = jnp.broadcast_to(mine[:, k : k + 1], (8, CELLS))

    own = core * 8 + chip

    def keep(source, k):
        for m in range(ROWS // 8):
            saved[pl.ds(k * ROWS + m * 8, 8), :] = source[pl.ds(m * 8 * LAYERS + own, 8, stride=LAYERS), :]

    keep(one, 0)

    def advance(turn, carry):
        apply_operator(one, two, index_ref)
        keep(two, 2 * turn + 1)
        apply_operator(two, one, index_ref)
        keep(one, 2 * turn + 2)
        return carry

    lax.fori_loop(0, DEGREE // 2, advance, 0)

    group = 16

    def combine(g, carry):
        total = [[None] * group for _ in range(3)]
        for k in range(DEGREE + 1):
            value = [saved[pl.ds(k * ROWS + (g * group + i) * 8, 8), :] for i in range(group)]
            for m in range(3):
                factor = spread_ref[pl.ds((k * 3 + m) * 8, 8), :]
                for i in range(group):
                    term = factor * value[i]
                    total[m][i] = term if total[m][i] is None else total[m][i] + term
        for m in range(3):
            for i in range(group):
                sum_ref[pl.ds(m * ROWS + (g * group + i) * 8, 8), :] = total[m][i]
        return carry

    lax.fori_loop(0, ROWS // 8 // group, combine, 0)
    table = table_ref[...]
    for m in range(3 * FIELDS):
        rows = pl.ds(m * NODES, NODES)
        out_ref[rows, :] = jnp.dot(
            table, sum_ref[rows, :], precision=lax.Precision.HIGHEST, preferred_element_type=jnp.float32
        )


def shards(initial, neighbours, step_counts):
    to_modes, to_nodes = modal_tables()
    axes = ("tm", "space")
    swap = route(lambda x, high, y, low, core: (x, high, y, low, core + 1))
    one_way = route(lambda x, high, y, low, core: (x, high, y, low, 1) if core == 0 else None)
    far = lax.ppermute(step_counts, axes, route(lambda x, high, y, low, core: (x + 2, high, y, low, core)))
    state = initial.reshape(ROWS, CELLS)
    other = lax.ppermute(state, axes, swap)
    near_other = lax.ppermute(neighbours, axes, swap)
    whole = lambda: pl.BlockSpec(memory_space=pltpu.VMEM)
    anywhere = lambda: pl.BlockSpec(memory_space=pl.ANY)
    scalar = lambda: pl.BlockSpec(memory_space=pltpu.SMEM)
    pair, late = pl.pallas_call(
        prepare_kernel,
        out_shape=[jax.ShapeDtypeStruct((PAIR, CELLS), jnp.float32)] * 2,
        in_specs=[scalar()] + [whole() for _ in range(5)],
        out_specs=[whole(), whole()],
    )(step_counts, state, other, neighbours, near_other, jnp.asarray(to_modes))
    late = pl.pallas_call(
        count_kernel,
        out_shape=jax.ShapeDtypeStruct((PAIR, CELLS), jnp.float32),
        in_specs=[scalar(), scalar(), anywhere()],
        out_specs=anywhere(),
        scratch_shapes=[pltpu.VMEM((8, CELLS), jnp.float32), pltpu.SemaphoreType.DMA],
        input_output_aliases={2: 0},
    )(step_counts, far, late)

    direct = []
    for k, entry in enumerate(OFFSETS):

        def move(x, high, y, low, core):
            if entry[core] is None:
                return None
            (step_y, step_z), (skew_x, skew_z) = entry[core]
            return (x + skew_x, high + skew_z, y + step_y, low + step_z, core)

        direct.append(lax.ppermute(pair if k < EARLY else late, axes, route(move)))
    own = lax.ppermute(late, axes, swap)
    swapped = [
        lax.ppermute(value, axes, one_way if entry[1] is None else swap) for value, entry in zip(direct, OFFSETS)
    ]
    pairs = [own] + direct + swapped

    result = pl.pallas_call(
        advance_kernel,
        out_shape=jax.ShapeDtypeStruct((3 * ROWS, CELLS), jnp.float32),
        in_specs=[whole() for _ in range(10)],
        out_specs=whole(),
        scratch_shapes=[
            pltpu.VMEM((ROWS * LAYERS, CELLS), jnp.float32),
            pltpu.VMEM((ROWS * LAYERS, CELLS), jnp.float32),
            pltpu.VMEM((6 * LAYERS, CELLS), jnp.int32),
            pltpu.VMEM(((DEGREE + 1) * ROWS, CELLS), jnp.float32),
            pltpu.VMEM((SLICES * 3 * 8, CELLS), jnp.float32),
            pltpu.VMEM(((DEGREE + 1) * 3 * 8, CELLS), jnp.float32),
            pltpu.VMEM((3 * ROWS, CELLS), jnp.float32),
        ],
        compiler_params=pltpu.CompilerParams(vmem_limit_bytes=32 * 1024 * 1024),
    )(*pairs, jnp.asarray(to_nodes))
    return result.reshape(1, 3, FIELDS, NODES, 1, CELLS)


def solution(mesh):
    placed = (P(None, None, "space", None), P(None, "space", None), P("tm"))
    return jax.shard_map(
        shards,
        mesh=mesh,
        in_specs=placed,
        out_specs=P("tm", None, None, None, "space", None),
        check_vma=False,
    )
```

```python
import functools

import jax
import jax.numpy as jnp
import numpy as np
from jax import lax
from jax.experimental import pallas as pl
from jax.experimental.pallas import tpu as pltpu
from jax.sharding import PartitionSpec as P

ORDER = 4
NODES = 64
ITERS = 2
FIELDS = 4
SLICES = 8
LAYERS = 16
CELLS = 128
ROWS = FIELDS * NODES
PART = ROWS + 8
PAIR = 2 * PART + 8
DEGREE = 22
BASE_STEP = 0.015

OFFSETS = (
    (((2, 1), (0, 0)), ((2, 0), (0, 0))),
    (((1, 0), (0, 0)), ((3, 0), (0, 0))),
    (((1, 1), (1, 1)), ((3, 1), (1, 0))),
    (((0, 1), (0, 1)), None),
)
EARLY = 2


def modal_tables():
    points = np.array([-1.0, -1.0 / np.sqrt(5.0), 1.0 / np.sqrt(5.0), 1.0])
    to_nodes = np.polynomial.legendre.legvander(points, ORDER - 1)
    to_modes = np.linalg.inv(to_nodes)
    cube = lambda m: np.kron(np.kron(m, m), m).astype(np.float32)
    return cube(to_modes), cube(to_nodes)


def route(move):
    pairs = []
    for x in range(4):
        for high in range(2):
            for y in range(4):
                for low in range(2):
                    for core in range(2):
                        target = move(x, high, y, low, core)
                        if target is None:
                            continue
                        to_x, to_high, to_y, to_low, to_core = target
                        source = (x * 2 + high) * 16 + y * 4 + low * 2 + core
                        place = (to_x % 4 * 2 + to_high % 2) * 16 + to_y % 4 * 4 + to_low % 2 * 2 + to_core % 2
                        pairs.append((source, place))
    return pairs


def prepare_kernel(step_ref, state_ref, other_ref, near_ref, near_other_ref, table_ref, out_ref, copy_ref):
    table = table_ref[...]
    core = lax.axis_index("space") % 2
    for k, (state, near) in enumerate(((state_ref, near_ref), (other_ref, near_other_ref))):
        base = pl.multiple_of((core if k == 0 else 1 - core) * PART, 8)
        for field in range(FIELDS):
            value = jnp.dot(
                table,
                state[pl.ds(field * NODES, NODES), :],
                precision=lax.Precision.HIGHEST,
                preferred_element_type=jnp.float32,
            )
            rows = pl.ds(base + field * NODES, NODES)
            out_ref[rows, :] = value
            copy_ref[rows, :] = value
        tail = jnp.concatenate([near[f].astype(jnp.float32) for f in (0, 1, 2, 3, 4, 5, 5, 5)], axis=0)
        rows = pl.ds(base + ROWS, 8)
        out_ref[rows, :] = tail
        copy_ref[rows, :] = tail
    lane = lax.broadcasted_iota(jnp.int32, (8, CELLS), 1)
    count = jnp.where(lane == lax.axis_index("tm"), step_ref[0], 0).astype(jnp.float32)
    out_ref[pl.ds(2 * PART, 8), :] = count
    copy_ref[pl.ds(2 * PART, 8), :] = count


def count_kernel(step_ref, far_ref, pair_any, out_any, counts, sem):
    lane = lax.broadcasted_iota(jnp.int32, (8, CELLS), 1)
    own = lax.axis_index("tm")
    far = (own // 2 + 2) % 4 * 2 + own % 2
    count = jnp.where(lane == own, step_ref[0], jnp.where(lane == far, far_ref[0], 0))
    counts[...] = count.astype(jnp.float32)
    copy = pltpu.make_async_copy(counts, out_any.at[pl.ds(2 * PART, 8), :], sem)
    copy.start()
    copy.wait()


def ends(p, u):
    o_p, o_u = p[1] + p[3], u[1] + u[3]
    m = (u[0] + u[2]) + o_p
    n = (p[0] + p[2]) + o_u
    return m - n, m + n, o_p, o_u


def rates(p, u, near_x, near_y, end):
    x, y, o_p, o_u = end
    d_x = near_x - x
    d_y = near_y - y
    p_0 = 0.25 * (d_y - d_x)
    u_0 = 0.25 * (d_x + d_y)
    t = u_0 + o_p
    w = p_0 + o_u
    rate_p = [p_0, -3.0 * (t + u[1]), 5.0 * (p_0 + u[0]), -3.0 * t]
    rate_u = [u_0, -3.0 * (w + p[1]), 5.0 * (u_0 + p[0]), -3.0 * w]
    return rate_p, rate_u


def lanes(value, index):
    return jnp.take_along_axis(value, index, axis=1, mode="promise_in_bounds")


def row(field, a, b, c, v):
    return (field * NODES + a * 16 + b * 4 + c) * LAYERS + v * 8


def apply_operator(src, dst, index_ref):
    get = lambda r: src[pl.ds(r, 8), :]

    def put(r, value):
        dst[pl.ds(r, 8), :] = value

    index = lambda face, v: index_ref[pl.ds(face * LAYERS + v * 8, 8), :]
    four = range(ORDER)
    middle = (1, 2)
    for b in four:
        end = [
            [ends([get(row(0, a, b, c, v)) for a in four], [get(row(1, a, b, c, v)) for a in four]) for c in four]
            for v in range(2)
        ]
        near_x = [
            [lanes(end[1][c][0], index(1, 0)) for c in four],
            [lanes(pltpu.roll(end[0][c][0], 7, 0), index(1, 1)) for c in four],
        ]
        near_y = [
            [lanes(pltpu.roll(end[1][c][1], 1, 0), index(0, 0)) for c in four],
            [lanes(end[0][c][1], index(0, 1)) for c in four],
        ]
        for v in range(2):
            for c in four:
                p = [get(row(0, a, b, c, v)) for a in middle]
                u = [get(row(1, a, b, c, v)) for a in middle]
                rate_p, rate_u = rates(p, u, near_x[v][c], near_y[v][c], end[v][c])
                for a in four:
                    put(row(0, a, b, c, v), rate_p[a])
                    put(row(1, a, b, c, v), rate_u[a])
    for v in range(2):
        for a in four:
            p = [[get(row(0, a, b, c, v)) for c in four] for b in four]
            rate = [[None] * ORDER for _ in four]
            end = [ends([p[b][c] for b in four], [get(row(2, a, b, c, v)) for b in four]) for c in four]
            near_x = [lanes(end[c][0], index(3, v)) for c in four]
            near_y = [lanes(end[c][1], index(2, v)) for c in four]
            for c in four:
                u = [get(row(2, a, b, c, v)) for b in middle]
                rate_p, rate_u = rates([p[b][c] for b in middle], u, near_x[c], near_y[c], end[c])
                for b in four:
                    rate[b][c] = rate_p[b]
                    put(row(2, a, b, c, v), rate_u[b])
            end = [ends(p[b], [get(row(3, a, b, c, v)) for c in four]) for b in four]
            near_x = [lanes(end[b][0], index(5, v)) for b in four]
            near_y = [lanes(end[b][1], index(4, v)) for b in four]
            for b in four:
                u = [get(row(3, a, b, c, v)) for c in middle]
                rate_p, rate_u = rates([p[b][c] for c in middle], u, near_x[b], near_y[b], end[b])
                for c in four:
                    r = row(0, a, b, c, v)
                    put(r, dst[pl.ds(r, 8), :] + (rate[b][c] + rate_p[c]))
                    put(row(3, a, b, c, v), rate_u[c])


def coefficients(counts):
    lane = lax.broadcasted_iota(jnp.int32, (8, CELLS), 1)
    wide = jnp.broadcast_to(counts, (8, CELLS))
    steps = [jnp.broadcast_to(wide[:, n : n + 1], (8, CELLS)) * BASE_STEP for n in range(SLICES)]
    image = lambda value: pltpu.roll(value, 1, 1)
    twice = lambda value: pltpu.roll(value, 2, 1)
    initial = jnp.where(lane == 0, 1.0, 0.0)
    states = [(initial, initial, initial)] * SLICES
    for _ in range(ITERS):
        begin = initial
        fresh = []
        for n in range(SLICES):
            h = steps[n]
            u_0, u_1, u_2 = states[n]
            old_0, old_1, old_2 = image(u_0), image(u_1), image(u_2)
            first = u_0 + h * (5.0 / 24.0 * old_0 + 1.0 / 3.0 * old_1 - 1.0 / 24.0 * old_2)
            image_first = image(first)
            second = (
                first
                + h * (image_first - old_1)
                + h * (-1.0 / 24.0 * old_0 + 1.0 / 3.0 * old_1 + 5.0 / 24.0 * old_2)
            )
            image_second = image(second)
            correction = h * (2.0 / 3.0 * image_first - 1.0 / 3.0 * old_0 - 1.0 / 3.0 * image_second)
            carried = h * (0.5 * image_second - 0.5 * old_0) + correction
            offset = 0.5 * h * image(carried) + correction
            finish = begin + h * image(begin) + 0.5 * h * h * twice(begin) + offset
            fresh.append((begin, first + 0.5 * ((begin - u_0) + (finish - second)), finish))
            begin = finish
        states = fresh
    return states


def advance_kernel(*refs):
    pairs = refs[:9]
    table_ref, out_ref, one, two, index_ref, saved, coef_ref, spread_ref, sum_ref = refs[9:]
    space = lax.axis_index("space")
    core = space % 2
    chip = space // 2
    low = chip % 2
    high = chip // 2
    counts = jnp.zeros((1, CELLS), jnp.float32)

    def take(read, step_y, step_z):
        place = (high + 4 - step_y) % 4 * 2 + (low + step_z) % 2
        for half in range(2):
            base = place + 8 * half
            for m in range(ROWS // 8):
                one[pl.ds(m * 8 * LAYERS + base, 8, stride=LAYERS), :] = read(half * PART + m * 8)
            tail = read(half * PART + ROWS)
            for face in range(6):
                index_ref[pl.ds(face * LAYERS + base, 1), :] = tail[face : face + 1].astype(jnp.int32)

    def reader(*sources):
        return lambda r: functools.reduce(jnp.add, [source[pl.ds(r, 8), :] for source in sources])

    take(reader(pairs[0]), 0, 0)
    for k, (zero, first) in enumerate(OFFSETS):
        if first is None:
            take(reader(pairs[1 + k], pairs[5 + k]), *zero[0])
        else:
            for swapped in range(2):
                on_zero = core == swapped
                step_y = jnp.where(on_zero, zero[0][0], first[0][0])
                step_z = jnp.where(on_zero, zero[0][1], first[0][1])
                take(reader(pairs[1 + 4 * swapped + k]), step_y, step_z)
    for pair in pairs:
        counts = jnp.maximum(counts, pair[pl.ds(2 * PART, 1), :])

    polynomials = coefficients(counts)
    for n in range(SLICES):
        for m in range(3):
            coef_ref[pl.ds((n * 3 + m) * 8, 8), :] = polynomials[n][m]
    own_slice = lax.axis_index("tm")
    for m in range(3):
        mine = coef_ref[pl.ds(pl.multiple_of((own_slice * 3 + m) * 8, 8), 8), :]
        for k in range(DEGREE + 1):
            spread_ref[pl.ds((k * 3 + m) * 8, 8), :] = jnp.broadcast_to(mine[:, k : k + 1], (8, CELLS))

    own = core * 8 + chip

    def keep(source, k):
        for m in range(ROWS // 8):
            saved[pl.ds(k * ROWS + m * 8, 8), :] = source[pl.ds(m * 8 * LAYERS + own, 8, stride=LAYERS), :]

    keep(one, 0)

    def advance(turn, carry):
        apply_operator(one, two, index_ref)
        keep(two, 2 * turn + 1)
        apply_operator(two, one, index_ref)
        keep(one, 2 * turn + 2)
        return carry

    lax.fori_loop(0, DEGREE // 2, advance, 0)

    group = 8

    def combine(g, carry):
        total = [[None] * group for _ in range(3)]
        for k in range(DEGREE + 1):
            value = [saved[pl.ds(k * ROWS + (g * group + i) * 8, 8), :] for i in range(group)]
            for m in range(3):
                factor = spread_ref[pl.ds((k * 3 + m) * 8, 8), :]
                for i in range(group):
                    term = factor * value[i]
                    total[m][i] = term if total[m][i] is None else total[m][i] + term
        for m in range(3):
            for i in range(group):
                sum_ref[pl.ds(m * ROWS + (g * group + i) * 8, 8), :] = total[m][i]
        return carry

    lax.fori_loop(0, ROWS // 8 // group, combine, 0)
    table = table_ref[...]
    for m in range(3 * FIELDS):
        rows = pl.ds(m * NODES, NODES)
        out_ref[rows, :] = jnp.dot(
            table, sum_ref[rows, :], precision=lax.Precision.HIGHEST, preferred_element_type=jnp.float32
        )


def shards(initial, neighbours, step_counts):
    to_modes, to_nodes = modal_tables()
    axes = ("tm", "space")
    swap = route(lambda x, high, y, low, core: (x, high, y, low, core + 1))
    one_way = route(lambda x, high, y, low, core: (x, high, y, low, 1) if core == 0 else None)
    far = lax.ppermute(step_counts, axes, route(lambda x, high, y, low, core: (x + 2, high, y, low, core)))
    state = initial.reshape(ROWS, CELLS)
    other = lax.ppermute(state, axes, swap)
    near_other = lax.ppermute(neighbours, axes, swap)
    whole = lambda: pl.BlockSpec(memory_space=pltpu.VMEM)
    anywhere = lambda: pl.BlockSpec(memory_space=pl.ANY)
    scalar = lambda: pl.BlockSpec(memory_space=pltpu.SMEM)
    pair, late = pl.pallas_call(
        prepare_kernel,
        out_shape=[jax.ShapeDtypeStruct((PAIR, CELLS), jnp.float32)] * 2,
        in_specs=[scalar()] + [whole() for _ in range(5)],
        out_specs=[whole(), whole()],
    )(step_counts, state, other, neighbours, near_other, jnp.asarray(to_modes))
    late = pl.pallas_call(
        count_kernel,
        out_shape=jax.ShapeDtypeStruct((PAIR, CELLS), jnp.float32),
        in_specs=[scalar(), scalar(), anywhere()],
        out_specs=anywhere(),
        scratch_shapes=[pltpu.VMEM((8, CELLS), jnp.float32), pltpu.SemaphoreType.DMA],
        input_output_aliases={2: 0},
    )(step_counts, far, late)

    direct = []
    for k, entry in enumerate(OFFSETS):

        def move(x, high, y, low, core):
            if entry[core] is None:
                return None
            (step_y, step_z), (skew_x, skew_z) = entry[core]
            return (x + skew_x, high + skew_z, y + step_y, low + step_z, core)

        direct.append(lax.ppermute(pair if k < EARLY else late, axes, route(move)))
    own = lax.ppermute(late, axes, swap)
    swapped = [
        lax.ppermute(value, axes, one_way if entry[1] is None else swap) for value, entry in zip(direct, OFFSETS)
    ]
    pairs = [own] + direct + swapped

    result = pl.pallas_call(
        advance_kernel,
        out_shape=jax.ShapeDtypeStruct((3 * ROWS, CELLS), jnp.float32),
        in_specs=[whole() for _ in range(10)],
        out_specs=whole(),
        scratch_shapes=[
            pltpu.VMEM((ROWS * LAYERS, CELLS), jnp.float32),
            pltpu.VMEM((ROWS * LAYERS, CELLS), jnp.float32),
            pltpu.VMEM((6 * LAYERS, CELLS), jnp.int32),
            pltpu.VMEM(((DEGREE + 1) * ROWS, CELLS), jnp.float32),
            pltpu.VMEM((SLICES * 3 * 8, CELLS), jnp.float32),
            pltpu.VMEM(((DEGREE + 1) * 3 * 8, CELLS), jnp.float32),
            pltpu.VMEM((3 * ROWS, CELLS), jnp.float32),
        ],
        compiler_params=pltpu.CompilerParams(vmem_limit_bytes=32 * 1024 * 1024),
    )(*pairs, jnp.asarray(to_nodes))
    return result.reshape(1, 3, FIELDS, NODES, 1, CELLS)


def solution(mesh):
    placed = (P(None, None, "space", None), P(None, "space", None), P("tm"))
    return jax.shard_map(
        shards,
        mesh=mesh,
        in_specs=placed,
        out_specs=P("tm", None, None, None, "space", None),
        check_vma=False,
    )
```
